256 devices in a mesh: branch: 2 (over x_lo), head: 4 (over y), tokens: 32 (over z, x_hi, core).
Axes of the slice: x: 4 (x_hi: 2, x_lo: 2; x = x_hi * 2 + x_lo), y: 4, z: 8, core: 2. Of those that a mesh axis runs over, the one named last changes fastest.
Arguments:
- queries: bfloat16 [2, 36864, 1536], P('branch', 'tokens', 'head'), may hold values from -128 to 128
- keys: bfloat16 [2, 36864, 1536], P('branch', 'tokens', 'head'), may hold values from -4 to 4
- values: bfloat16 [2, 36864, 1536], P('branch', 'tokens', 'head'), may hold values from -96 to 96
- residual: bfloat16 [2, 36864, 2, 1536], P('branch', 'tokens', None, 'head'), may hold values from -3 to 3
- gate: bfloat16 [2, 2, 1536], replicated, may hold values from 0.099609375 to 1.8984375
- out_weight: bfloat16 [1536, 3072], P('head'), may hold values from -0.15625 to 0.15625
- time_offsets: int32 [3, 32], replicated, may hold values from 0 to 1
- guidance_index: int32 [18], replicated, may hold values from 0 to 7
Outputs:
- guided: bfloat16 [36864, 3072], P('tokens', ('branch', 'head'))
The draws below stay inside these ranges and needn't reach their ends.
All inputs are finite; a program needn't handle non-finite values.
Results may differ from the reference program's by a relative error of at most 0.0051.
Values may be sent and summed in bfloat16 or wider, within the bound.
A program may use at most 128 MiB of HBM per device.

```python
import math
import jax
import jax.numpy as jnp
from jax import lax

D = 3072
HEADS = 12
HD = 128
ATT = 1536
TH = 8
TW = 8
TILES_T = 3
TILE = 384
TILES_W = 32
FRAMES = 18
TOKENS = 36864


def shared_keys(key):
    base_keys = jax.random.normal(key, (2, TOKENS, ATT), jnp.float32)
    return jnp.clip(base_keys, -4.0, 4.0)


def draw_keys(key, part):
    base_keys = shared_keys(key)
    return base_keys.astype(jnp.bfloat16)


def draw_queries(key, part):
    key = jax.random.fold_in(key, 2)
    fresh_rows = jnp.clip(jax.random.normal(key, (2, TOKENS, ATT), jnp.float32), -4.0, 4.0)
    return fresh_rows.astype(jnp.bfloat16)


def touch_ends(array, key, low, high):
    longest = array.shape.index(max(array.shape))
    spots = []
    for shift in (0, 1):
        where = [jax.random.randint(jax.random.fold_in(key, axis), (), 0, length) for axis, length in enumerate(array.shape)]
        where[longest] = (where[longest] + shift) % array.shape[longest]
        spots.append(tuple(where))
    return array.at[spots[0]].set(low).at[spots[1]].set(high)


def block_scale(key, dims, split, low, largest):
    level = 1.0
    for dim, parts in split:
        heights = jax.random.uniform(jax.random.fold_in(jax.random.fold_in(key, 6), dim), (parts,), jnp.float32, low / len(split), largest / len(split))
        level = level * jnp.repeat(jnp.exp(heights), dims[dim] // parts).reshape((-1,) + (1,) * (len(dims) - 1 - dim))
    return level


def bell_draw(rng, extent, spread, most, split=(), held_as=jnp.bfloat16):
    array = spread * jax.random.normal(rng, extent, jnp.float32)
    if split:
        array = array * block_scale(rng, extent, split, -0.22, 0.18)
    return jnp.clip(array, -most, most).astype(held_as)


def setup_inputs(seed: int = 0) -> dict:
    splits = jax.random.split(jax.random.key(seed), 9)
    queries = draw_queries(jax.random.fold_in(splits[8], 71), 0)
    keys = draw_keys(jax.random.fold_in(splits[8], 71), 0)
    values = bell_draw(splits[2], (2, TOKENS, ATT), 16.0, 96.0, ((0, 2), (1, 32), (2, 4)))
    residual = bell_draw(splits[3], (2, TOKENS, 2, D // 2), 0.5, 3.0, ((0, 2), (1, 32), (3, 4)))
    gate = jnp.clip(1.0 + 0.18 * jax.random.normal(splits[4], (2, 2, D // 2), jnp.float32), 0.099609375, 1.8984375).astype(jnp.bfloat16)
    out_weight = bell_draw(splits[5], (ATT, D), ATT ** -0.5, 0.15625, ((0, 4),))
    time_offsets = touch_ends(jax.random.randint(splits[6], (TILES_T, TILES_W), 0, 2), jax.random.fold_in(splits[6], 1), 0, 1).astype(jnp.int32)
    guidance_index = touch_ends(jax.random.randint(splits[7], (FRAMES,), 0, 8), jax.random.fold_in(splits[7], 1), 0, 7).astype(jnp.int32)
    return dict(queries=queries, keys=keys, values=values, residual=residual, gate=gate, out_weight=out_weight, time_offsets=time_offsets, guidance_index=guidance_index)


def reference(queries, keys, values, residual, gate, out_weight, time_offsets, guidance_index):
    tile_shape = (2, TILES_W, TILES_T, TILE, HEADS, HD)
    query_tiles = queries.reshape(tile_shape)
    key_tiles = keys.reshape(tile_shape)
    value_tiles = values.reshape(tile_shape)
    tile_count = TILES_W * TILES_T
    score_scale = 1.0 / math.sqrt(HD)
    near_steps = jnp.arange(3, dtype=jnp.int32) - 1
    time_range = jnp.arange(TILES_T, dtype=jnp.int32)

    def one_tile(tile_index):
        branch = tile_index // tile_count
        tile_rest = tile_index % tile_count
        width_tile = tile_rest // TILES_T
        time_tile = tile_rest % TILES_T
        query_tile = query_tiles[branch, width_tile, time_tile].astype(jnp.float32)
        width_near = width_tile + near_steps
        width_safe = jnp.clip(width_near, 0, TILES_W - 1).astype(jnp.int32)
        key_block = jnp.take(key_tiles[branch], width_safe, axis=0)
        value_block = jnp.take(value_tiles[branch], width_safe, axis=0)
        offset = time_offsets[time_tile, width_tile]
        time_ok = (time_range >= time_tile - offset) & (time_range <= time_tile - offset + 1)
        width_ok = (width_near >= 0) & (width_near < TILES_W)
        allowed = width_ok[:, None, None] & time_ok[None, :, None]
        allowed = jnp.broadcast_to(allowed, (3, TILES_T, TILE)).reshape(-1)
        key_flat = key_block.reshape(-1, HEADS, HD).astype(jnp.float32)
        value_flat = value_block.reshape(-1, HEADS, HD).astype(jnp.float32)
        scores = jnp.einsum('qhd,khd->hqk', query_tile, key_flat) * score_scale
        masked = jnp.where(allowed[None, None, :], scores, -1e+30)
        row_max = lax.optimization_barrier(jnp.max(masked, axis=2, keepdims=True))
        weights = jnp.where(allowed[None, None, :], jnp.exp(masked - row_max), 0.0)
        norm_total = lax.optimization_barrier(jnp.sum(weights, axis=2, keepdims=True))
        rounded = lax.optimization_barrier(weights.astype(jnp.bfloat16)).astype(jnp.float32)
        blended = jnp.einsum('hqk,khd->qhd', rounded, value_flat)
        return (blended / jnp.transpose(norm_total, (1, 0, 2))).reshape(TILE, ATT).astype(jnp.bfloat16)
    attention = lax.map(one_tile, jnp.arange(2 * tile_count, dtype=jnp.int32)).reshape(2, TOKENS, ATT)
    projected = jnp.stack([jnp.dot(attention[0], out_weight, preferred_element_type=jnp.float32), jnp.dot(attention[1], out_weight, preferred_element_type=jnp.float32)])
    residual_flat = residual.reshape(2, TOKENS, D).astype(jnp.float32)
    gate_flat = gate.reshape(2, D).astype(jnp.float32)
    hidden = residual_flat + gate_flat[:, None, :] * projected
    guide_scale = 1.0 + 0.5 * guidance_index.astype(jnp.float32)
    token_scale = jnp.broadcast_to(guide_scale.reshape(1, FRAMES, 1), (TILES_W, FRAMES, TH * TW)).reshape(TOKENS)
    guided = hidden[1] + token_scale[:, None] * (hidden[0] - hidden[1])
    return guided.astype(jnp.bfloat16)
```

```python
import math

import jax
import jax.numpy as jnp
from jax import lax
from jax.experimental import pallas as pl
from jax.experimental.pallas import tpu as pltpu
from jax.sharding import PartitionSpec as P

HD = 128
TILE = 384
FRAME = 64
BF = jnp.bfloat16
F32 = jnp.float32
SCALE = math.log2(math.e) / math.sqrt(HD)
WINDOW = 3
PIECES = 9


def kernel(
    offsets, guidance, gate, q_hbm, k_hbm, v_hbm, r_hbm, w_hbm, out_hbm,
    q_own, k_own, v_own, k_left, v_left, k_right, v_right, res, w_all, att, scores,
    own_half, x_send, x_recv, out_v,
    local_sem, halo_send, halo_recv, w_send, w_recv, a_send, a_recv, x_ssem, x_rsem, out_sem,
):
    branch = lax.axis_index("branch")
    head = lax.axis_index("head")
    width = lax.axis_index("tokens")
    widths = lax.axis_size("tokens")
    heads = lax.axis_size("head")
    features = q_own.shape[1]
    local_heads = features // HD
    tiles = q_own.shape[0] // TILE
    half_full = w_hbm.shape[1] // 2
    has_left = width > 0
    has_right = width < widths - 1
    peers = [lax.rem(head + d, heads) for d in range(1, heads)]

    def mine_columns(which, owner):
        half = branch if which == 0 else 1 - branch
        return pl.ds(pl.multiple_of(half * half_full + owner * features, HD), features)

    loads = [
        pltpu.make_async_copy(src, dst, local_sem.at[i])
        for i, (src, dst) in enumerate(
            ((k_hbm, k_own), (v_hbm, v_own), (q_hbm, q_own), (r_hbm, res))
        )
    ] + [
        pltpu.make_async_copy(
            w_hbm.at[:, mine_columns(which, head)],
            w_all.at[0, :, pl.ds(which * features, features)],
            local_sem.at[4 + which],
        )
        for which in range(2)
    ]
    for load in loads:
        load.start()

    barrier = pltpu.get_barrier_semaphore()

    @pl.when(has_left)
    def _():
        pl.semaphore_signal(barrier, inc=1, device_id={"tokens": width - 1})

    @pl.when(has_right)
    def _():
        pl.semaphore_signal(barrier, inc=1, device_id={"tokens": width + 1})

    for peer in peers:
        pl.semaphore_signal(barrier, inc=1, device_id={"head": peer})
    pl.semaphore_signal(barrier, inc=1, device_id={"branch": 1 - branch})
    pl.semaphore_wait(
        barrier, heads + has_left.astype(jnp.int32) + has_right.astype(jnp.int32)
    )

    def piece(index):
        early = index < 2 * local_heads
        tile = jnp.where(early, lax.rem(index, 2), 2)
        own_head = jnp.where(early, index // 2, index - 2 * local_heads)
        return (
            pl.ds(pl.multiple_of(tile * TILE, TILE), TILE),
            pl.ds(pl.multiple_of(own_head * HD, HD), HD),
        )

    def halo_copies(index, leftwards):
        where = piece(index)
        target = width - 1 if leftwards else width + 1
        place = 0 if leftwards else 2
        dests = (k_right, v_right) if leftwards else (k_left, v_left)
        return [
            pltpu.make_async_remote_copy(
                src_ref=src.at[where],
                dst_ref=dst.at[where],
                send_sem=halo_send.at[index, place + i],
                recv_sem=halo_recv.at[index, place + i],
                device_id={"tokens": target},
            )
            for i, (src, dst) in enumerate(zip((k_hbm, v_hbm), dests))
        ]

    def send_piece(index):
        @pl.when(has_left)
        def _():
            for copy in halo_copies(index, True):
                copy.start()

        @pl.when(has_right)
        def _():
            for copy in halo_copies(index, False):
                copy.start()

    def take_piece(index):
        @pl.when(has_right)
        def _():
            for copy in halo_copies(index, True):
                copy.wait_recv()

        @pl.when(has_left)
        def _():
            for copy in halo_copies(index, False):
                copy.wait_recv()

        @pl.when(index + WINDOW < PIECES)
        def _():
            send_piece(index + WINDOW)

    for index in range(WINDOW):
        send_piece(index)

    def w_copies(d):
        return [
            pltpu.make_async_remote_copy(
                src_ref=w_hbm.at[:, mine_columns(which, peers[d - 1])],
                dst_ref=w_all.at[heads - d, :, pl.ds(which * features, features)],
                send_sem=w_send.at[d - 1, which],
                recv_sem=w_recv.at[heads - d - 1, which],
                device_id={"head": peers[d - 1]},
            )
            for which in range(2)
        ]

    for d in range(1, heads):
        for copy in w_copies(d):
            copy.start()
    for load in loads:
        load.wait()

    @pl.when(jnp.logical_not(has_left))
    def _():
        k_left[...] = k_own[...]
        v_left[...] = jnp.zeros_like(v_left)

    @pl.when(jnp.logical_not(has_right))
    def _():
        k_right[...] = k_own[...]
        v_right[...] = jnp.zeros_like(v_right)

    columns = (
        (k_own, v_own, jnp.float32(1)),
        (k_left, v_left, has_left.astype(F32)),
        (k_right, v_right, has_right.astype(F32)),
    )

    def unit(tile, own_head):
        offset = offsets[tile, width]
        back = offset == 1
        second = jnp.where(back, tile - 1, tile + 1)
        valid = jnp.logical_and(second >= 0, second < tiles)
        rows = pl.ds(pl.multiple_of(tile * TILE, TILE), TILE)
        before = pl.ds(pl.multiple_of(jnp.maximum(tile - 1, 0) * TILE, TILE), TILE)
        after = pl.ds(pl.multiple_of(jnp.minimum(tile + 1, tiles - 1) * TILE, TILE), TILE)
        cols = pl.ds(pl.multiple_of(own_head * HD, HD), HD)
        query = q_own[rows, cols]
        top = None
        for i, (k_ref, _, _) in enumerate(columns):
            for which in range(2):
                if which == 0:
                    key = k_ref[rows, cols]
                else:
                    key = jnp.where(back, k_ref[before, cols], k_ref[after, cols])
                found = lax.dot_general(
                    query, key, (((1,), (1,)), ((), ())), preferred_element_type=F32
                )
                first = (2 * i + which) * TILE
                scores[:, first : first + TILE] = found
                for lane in range(0, TILE, HD):
                    part = found[:, lane : lane + HD]
                    top = part if top is None else jnp.maximum(top, part)
        top = jnp.max(top, axis=1, keepdims=True) * SCALE
        total = None
        for i, (_, v_ref, present) in enumerate(columns):
            for which in range(2):
                if which == 0:
                    value = v_ref[rows, cols]
                    count = present
                else:
                    value = jnp.where(back, v_ref[before, cols], v_ref[after, cols])
                    value = jnp.where(valid, value, jnp.zeros_like(value))
                    count = present * valid.astype(F32)
                ones = jnp.full((TILE, HD), count, F32).astype(BF)
                first = (2 * i + which) * TILE
                weights = jnp.exp2(scores[:, first : first + TILE] * SCALE - top).astype(BF)
                term = jnp.dot(
                    weights,
                    jnp.concatenate([value, ones], axis=1),
                    preferred_element_type=F32,
                )
                total = term if total is None else total + term
        att[0, rows, cols] = (total[:, :HD] / total[:, HD:]).astype(BF)

    def att_copies(tile, own_head):
        where = (
            pl.ds(pl.multiple_of(tile * TILE, TILE), TILE),
            pl.ds(pl.multiple_of(own_head * HD, HD), HD),
        )
        slot = tile * local_heads + own_head
        return [
            pltpu.make_async_remote_copy(
                src_ref=att.at[(0, *where)],
                dst_ref=att.at[(heads - d, *where)],
                send_sem=a_send.at[slot, d - 1],
                recv_sem=a_recv.at[slot, heads - d - 1],
                device_id={"head": peers[d - 1]},
            )
            for d in range(1, heads)
        ]

    def run_unit(tile, own_head):
        unit(tile, own_head)
        for copy in att_copies(tile, own_head):
            copy.start()

    @pl.loop(0, local_heads)
    def _(own_head):
        take_piece(2 * own_head)
        take_piece(2 * own_head + 1)
        run_unit(0, own_head)

    def exchange(tile):
        rows = pl.ds(tile * TILE, TILE)
        return pltpu.make_async_remote_copy(
            src_ref=x_send.at[rows],
            dst_ref=x_recv.at[rows],
            send_sem=x_ssem.at[tile],
            recv_sem=x_rsem.at[tile],
            device_id={"branch": 1 - branch},
        )

    gate_cols = pl.ds(pl.multiple_of(head * features, HD), features)

    def project(tile):
        rows = pl.ds(tile * TILE, TILE)
        for own_head in range(local_heads):
            for copy in att_copies(tile, own_head):
                copy.wait_recv()
        for which in (1, 0):
            half = branch if which == 0 else 1 - branch
            lanes = pl.ds(which * features, features)
            summed = None
            for slot in range(heads):
                term = jnp.dot(
                    att[slot, rows, :], w_all[slot, :, lanes], preferred_element_type=F32
                )
                summed = term if summed is None else summed + term
            scale = gate[pl.ds(branch * 2 + half, 1), gate_cols]
            hidden = res[half, rows, :].astype(F32) + scale * summed
            if which == 1:
                x_send[rows, :] = hidden.astype(BF)
                exchange(tile).start()
            else:
                own_half[rows, :] = hidden

    def combine(tile):
        exchange(tile).wait_recv()
        frames = TILE // FRAME
        for frame in range(frames):
            rows = pl.ds(tile * TILE + frame * FRAME, FRAME)
            step = guidance[tile * frames + frame].astype(F32)
            strength = 1.0 + 0.5 * step
            mine = jnp.where(branch == 0, strength, 1.0 - strength)
            theirs = 1.0 - mine
            guided = own_half[rows, :] * mine + x_recv[rows, :].astype(F32) * theirs
            out_v[rows, :] = guided.astype(BF)
        rows = pl.ds(tile * TILE, TILE)
        pltpu.make_async_copy(out_v.at[rows], out_hbm.at[rows], out_sem.at[tile]).start()

    for own_head in range(local_heads):
        take_piece(jnp.int32(2 * local_heads + own_head))

        @pl.loop(1, tiles)
        def _(tile):
            run_unit(tile, own_head)

        if own_head == 0:
            for d in range(1, heads):
                for copy in w_copies(d):
                    copy.wait_recv()
            project(0)

    for tile in range(1, tiles):
        project(tile)
    for tile in range(tiles):
        combine(tile)

    for tile in range(tiles):
        rows = pl.ds(tile * TILE, TILE)
        pltpu.make_async_copy(out_v.at[rows], out_hbm.at[rows], out_sem.at[tile]).wait()
        exchange(tile).wait_send()
    for d in range(1, heads):
        for copy in w_copies(d):
            copy.wait_send()

    @pl.loop(0, PIECES)
    def _(index):
        for copy in att_copies(index // local_heads, lax.rem(index, local_heads)):
            copy.wait_send()

        @pl.when(has_left)
        def _():
            for copy in halo_copies(index, True):
                copy.wait_send()

        @pl.when(has_right)
        def _():
            for copy in halo_copies(index, False):
                copy.wait_send()


def local(queries, keys, values, residual, gate, out_weight, time_offsets, guidance_index):
    rows, features = queries.shape[1:]
    heads = lax.axis_size("head")
    halves = jnp.transpose(residual[0], (1, 0, 2))
    gates = gate.reshape(4, gate.shape[2]).astype(F32)
    smem = pl.BlockSpec(memory_space=pltpu.SMEM)
    vmem = pl.BlockSpec(memory_space=pltpu.VMEM)
    hbm = pl.BlockSpec(memory_space=pl.ANY)
    block = pltpu.VMEM((rows, features), BF)
    dma = pltpu.SemaphoreType.DMA
    tiles = rows // TILE
    return pl.pallas_call(
        kernel,
        out_shape=jax.ShapeDtypeStruct((rows, features), BF),
        in_specs=[smem, smem, vmem, hbm, hbm, hbm, hbm, hbm],
        out_specs=hbm,
        scratch_shapes=[block] * 7
        + [
            pltpu.VMEM((2, rows, features), BF),
            pltpu.VMEM((heads, features, 2 * features), BF),
            pltpu.VMEM((heads, rows, features), BF),
            pltpu.VMEM((TILE, 6 * TILE), F32),
            pltpu.VMEM((rows, features), F32),
            block,
            block,
            block,
            dma((6,)),
            dma((PIECES, 4)),
            dma((PIECES, 4)),
            dma((heads - 1, 2)),
            dma((heads - 1, 2)),
            dma((PIECES, heads - 1)),
            dma((PIECES, heads - 1)),
            dma((tiles,)),
            dma((tiles,)),
            dma((tiles,)),
        ],
        compiler_params=pltpu.CompilerParams(
            collective_id=0, has_side_effects=True, vmem_limit_bytes=48 * 2**20
        ),
        name="block",
    )(time_offsets, guidance_index, gates, queries[0], keys[0], values[0], halves, out_weight)


def solution(mesh):
    return jax.shard_map(
        local,
        mesh=mesh,
        in_specs=(
            P("branch", "tokens", "head"),
            P("branch", "tokens", "head"),
            P("branch", "tokens", "head"),
            P("branch", "tokens", None, "head"),
            P(),
            P("head", None),
            P(),
            P(),
        ),
        out_specs=P("tokens", ("branch", "head")),
        check_vma=False,
    )
```

```python
import math

import jax
import jax.numpy as jnp
from jax import lax
from jax.experimental import pallas as pl
from jax.experimental.pallas import tpu as pltpu
from jax.sharding import PartitionSpec as P

HD = 128
TILE = 384
FRAME = 64
BF = jnp.bfloat16
F32 = jnp.float32
SCALE = math.log2(math.e) / math.sqrt(HD)
WINDOW = 3
PIECES = 9
VMEM = 62 * 2**20
PIECE_ORDER = ((0, 0), (1, 0), (2, 0), (0, 1), (1, 1), (0, 2), (1, 2), (2, 1), (2, 2))
UNIT_ORDER = ((0, 0), (1, 0), (2, 0), (0, 1), (0, 2), (1, 1), (2, 1), (1, 2), (2, 2))
NEEDED = (2, 3, 3, 5, 7, 8, 8, 9, 9)
BEGUN = (2, 3, 3, 6, 9, 9, 9, 9, 9)
DIRECT = (4, 7, 8)
LAG = 2
SHARE_AT = 2
PROJECT_AT = 6


def pick(index, table, field=None):
    found = 0
    for i, entry in enumerate(table):
        value = entry if field is None else entry[field]
        if value:
            found = found + jnp.where(index == i, value, 0)
    return found


def kernel(
    offsets, guidance, gate, q_hbm, k_hbm, v_hbm, r_hbm, w_hbm, out_hbm,
    q_own, k_own, v_own, k_near, v_near, k_far, v_far, res_raw, res, w_all, att, scores, tops, totals,
    own_half, x_send, x_recv, out_v,
    local_sem, near_send, near_recv, halo_send, halo_recv, w_send, w_recv, s_send, s_recv, a_send, a_recv, x_ssem, x_rsem, out_sem,
):
    branch = lax.axis_index("branch")
    head = lax.axis_index("head")
    width = lax.axis_index("tokens")
    widths = lax.axis_size("tokens")
    heads = lax.axis_size("head")
    features = q_own.shape[1]
    local_heads = features // HD
    tiles = q_own.shape[0] // TILE
    half_full = w_hbm.shape[1] // 2
    rows_all = q_own.shape[0]
    step = 1 - 2 * lax.rem(width, 2)
    sibling = width + step
    far = width - step
    has_far = jnp.logical_and(far >= 0, far < widths)
    peers = [lax.rem(head + d, heads) for d in range(1, heads)]

    def mine_columns(which, owner):
        half = branch if which == 0 else 1 - branch
        return pl.ds(pl.multiple_of(half * half_full + owner * features, HD), features)

    loads = [
        pltpu.make_async_copy(src, dst, local_sem.at[i])
        for i, (src, dst) in enumerate(
            ((k_hbm, k_own), (v_hbm, v_own), (q_hbm, q_own), (r_hbm, res_raw))
        )
    ] + [
        pltpu.make_async_copy(
            w_hbm.at[:, mine_columns(which, head)],
            w_all.at[0, :, pl.ds(which * features, features)],
            local_sem.at[4 + which],
        )
        for which in range(2)
    ]
    for load in loads:
        load.start()

    barrier = pltpu.get_barrier_semaphore()

    @pl.when(has_far)
    def _():
        pl.semaphore_signal(barrier, inc=1, device_id={"tokens": far})

    pl.semaphore_signal(barrier, inc=1, device_id={"tokens": sibling})
    for peer in peers:
        pl.semaphore_signal(barrier, inc=1, device_id={"head": peer})
    pl.semaphore_signal(barrier, inc=1, device_id={"branch": 1 - branch})
    pl.semaphore_wait(barrier, heads + 1 + has_far.astype(jnp.int32))

    near_copies = [
        pltpu.make_async_remote_copy(
            src_ref=src,
            dst_ref=dst,
            send_sem=near_send.at[i],
            recv_sem=near_recv.at[i],
            device_id={"tokens": sibling},
        )
        for i, (src, dst) in enumerate(((k_hbm, k_near), (v_hbm, v_near)))
    ]

    def piece(index):
        tile, own_head = pick(index, PIECE_ORDER, 0), pick(index, PIECE_ORDER, 1)
        return (
            pl.ds(pl.multiple_of(tile * TILE, TILE), TILE),
            pl.ds(pl.multiple_of(own_head * HD, HD), HD),
        )

    def far_copies(index):
        where = piece(index)
        return [
            pltpu.make_async_remote_copy(
                src_ref=src.at[where],
                dst_ref=dst.at[where],
                send_sem=halo_send.at[index, i],
                recv_sem=halo_recv.at[index, i],
                device_id={"tokens": far},
            )
            for i, (src, dst) in enumerate(((k_hbm, k_far), (v_hbm, v_far)))
        ]

    def send_piece(index):
        @pl.when(has_far)
        def _():
            for copy in far_copies(index):
                copy.start()

    def take_piece(index):
        @pl.when(has_far)
        def _():
            for copy in far_copies(index):
                copy.wait_recv()

        @pl.when(index + WINDOW < PIECES)
        def _():
            send_piece(index + WINDOW)

    for index in range(WINDOW):
        send_piece(index)

    share = features // 2
    mine = pl.ds(pl.multiple_of(lax.rem(width, 2) * share, share), share)
    others = pl.ds(pl.multiple_of((1 - lax.rem(width, 2)) * share, share), share)

    def w_copies(d):
        return [
            pltpu.make_async_remote_copy(
                src_ref=w_hbm.at[mine, mine_columns(which, peers[d - 1])],
                dst_ref=w_all.at[heads - d, mine, pl.ds(which * features, features)],
                send_sem=w_send.at[d - 1, which],
                recv_sem=w_recv.at[heads - d - 1, which],
                device_id={"head": peers[d - 1]},
            )
            for which in range(2)
        ]

    def w_share(slot, rows):
        return pltpu.make_async_remote_copy(
            src_ref=w_all.at[slot, rows],
            dst_ref=w_all.at[slot, rows],
            send_sem=s_send.at[slot - 1],
            recv_sem=s_recv.at[slot - 1],
            device_id={"tokens": sibling},
        )

    for d in range(1, heads):
        for copy in w_copies(d):
            copy.start()
    for copy in near_copies:
        copy.start()
    for load in loads:
        load.wait()
    for part in range(rows_all // FRAME):
        span = pl.ds(part * FRAME, FRAME)
        both = res_raw[span, :, :].astype(F32)
        for half in range(2):
            res[half, span, :] = both[:, half, :].astype(BF)

    @pl.when(jnp.logical_not(has_far))
    def _():
        k_far[...] = k_own[...]
        v_far[...] = jnp.zeros_like(v_far)

    early = ((k_own, v_own), (k_near, v_near))
    late = ((k_far, v_far),)

    def attend(tile, own_head, columns, present):
        offset = offsets[tile, width]
        back = offset == 1
        second = jnp.where(back, tile - 1, tile + 1)
        valid = jnp.logical_and(second >= 0, second < tiles)
        rows = pl.ds(pl.multiple_of(tile * TILE, TILE), TILE)
        before = pl.ds(pl.multiple_of(jnp.maximum(tile - 1, 0) * TILE, TILE), TILE)
        after = pl.ds(pl.multiple_of(jnp.minimum(tile + 1, tiles - 1) * TILE, TILE), TILE)
        cols = pl.ds(pl.multiple_of(own_head * HD, HD), HD)
        query = q_own[rows, cols]
        top = None
        for i, (k_ref, _) in enumerate(columns):
            for which in range(2):
                if which == 0:
                    key = k_ref[rows, cols]
                else:
                    key = jnp.where(back, k_ref[before, cols], k_ref[after, cols])
                found = lax.dot_general(
                    query, key, (((1,), (1,)), ((), ())), preferred_element_type=F32
                )
                first = (2 * i + which) * TILE
                scores[:, first : first + TILE] = found
                for lane in range(0, TILE, HD):
                    part = found[:, lane : lane + HD]
                    top = part if top is None else jnp.maximum(top, part)
        top = jnp.max(top, axis=1, keepdims=True) * SCALE

        def blend(top):
            total = None
            for i, (_, v_ref) in enumerate(columns):
                for which in range(2):
                    if which == 0:
                        value = v_ref[rows, cols]
                        count = present
                    else:
                        value = jnp.where(back, v_ref[before, cols], v_ref[after, cols])
                        value = jnp.where(valid, value, jnp.zeros_like(value))
                        count = present * valid.astype(F32)
                    ones = jnp.full((TILE, HD), count, F32).astype(BF)
                    first = (2 * i + which) * TILE
                    weights = jnp.exp2(scores[:, first : first + TILE] * SCALE - top).astype(BF)
                    term = jnp.dot(
                        weights,
                        jnp.concatenate([value, ones], axis=1),
                        preferred_element_type=F32,
                    )
                    total = term if total is None else total + term
            return total

        return top, blend

    def begin_unit(index):
        tile, own_head = pick(index, UNIT_ORDER, 0), pick(index, UNIT_ORDER, 1)
        top, blend = attend(tile, own_head, early, jnp.float32(1))
        tops[index] = jnp.broadcast_to(top, (TILE, HD))
        totals[index] = blend(top)

    def end_unit(tile, own_head, index):
        top, blend = attend(tile, own_head, late, has_far.astype(F32))
        old = tops[index][:, :1]
        new = jnp.maximum(old, top)
        total = blend(new) + totals[index] * jnp.exp2(old - new)
        rows = pl.ds(pl.multiple_of(tile * TILE, TILE), TILE)
        cols = pl.ds(pl.multiple_of(own_head * HD, HD), HD)
        att[0, rows, cols] = (total[:, :HD] / total[:, HD:]).astype(BF)

    def gather_copy(tile, own_head, kind):
        forwards = kind % 2 == 0
        own = kind != 2 and kind != 3
        first = tile * TILE + (0 if own or forwards else TILE // 2)
        count = TILE if own else TILE // 2
        where = (
            pl.ds(pl.multiple_of(first, TILE // 2), count),
            pl.ds(pl.multiple_of(own_head * HD, HD), HD),
        )
        came = heads - 1 if forwards else 1
        source = 0 if own else came
        dest = came if kind < 2 else 2
        target = peers[1] if kind == 4 else peers[0] if forwards else peers[-1]
        index = tile * local_heads + own_head
        return pltpu.make_async_remote_copy(
            src_ref=att.at[(source, *where)],
            dst_ref=att.at[(dest, *where)],
            send_sem=a_send.at[index, kind],
            recv_sem=a_recv.at[index, kind],
            device_id={"head": target},
        )

    def relay(tile, own_head):
        for kind in (0, 1):
            gather_copy(tile, own_head, kind).wait_recv()
            gather_copy(tile, own_head, kind + 2).start()

    def share_weights():
        for d in range(1, heads):
            for copy in w_copies(d):
                copy.wait_recv()
        for slot in range(1, heads):
            w_share(slot, mine).start()

    def exchange(tile):
        rows = pl.ds(tile * TILE, TILE)
        return pltpu.make_async_remote_copy(
            src_ref=x_send.at[rows],
            dst_ref=x_recv.at[rows],
            send_sem=x_ssem.at[tile],
            recv_sem=x_rsem.at[tile],
            device_id={"branch": 1 - branch},
        )

    gate_cols = pl.ds(pl.multiple_of(head * features, HD), features)

    def project(tile):
        rows = pl.ds(tile * TILE, TILE)
        for own_head in range(local_heads):
            direct = UNIT_ORDER.index((tile, own_head)) in DIRECT
            for kind in (0, 1, 4) if direct else (2, 3):
                gather_copy(tile, own_head, kind).wait_recv()
        for which in (1, 0):
            half = branch if which == 0 else 1 - branch
            lanes = pl.ds(which * features, features)
            summed = None
            for slot in range(heads):
                term = jnp.dot(
                    att[slot, rows, :], w_all[slot, :, lanes], preferred_element_type=F32
                )
                summed = term if summed is None else summed + term
            both = gate[branch, :, gate_cols].astype(F32)
            scale = jnp.where(half == 0, both[0:1], both[1:2])
            hidden = res[half, rows, :].astype(F32) + scale * summed
            if which == 1:
                x_send[rows, :] = hidden.astype(BF)
                exchange(tile).start()
            else:
                own_half[rows, :] = hidden

    def combine(tile):
        exchange(tile).wait_recv()
        frames = TILE // FRAME
        for frame in range(frames):
            rows = pl.ds(tile * TILE + frame * FRAME, FRAME)
            step = guidance[tile * frames + frame].astype(F32)
            strength = 1.0 + 0.5 * step
            mine = jnp.where(branch == 0, strength, 1.0 - strength)
            theirs = 1.0 - mine
            guided = own_half[rows, :] * mine + x_recv[rows, :].astype(F32) * theirs
            out_v[rows, :] = guided.astype(BF)
        rows = pl.ds(tile * TILE, TILE)
        pltpu.make_async_copy(out_v.at[rows], out_hbm.at[rows], out_sem.at[tile]).start()

    for copy in near_copies:
        copy.wait_recv()

    @pl.loop(0, PIECES)
    def _(index):
        begun = jnp.where(index == 0, 0, pick(index - 1, BEGUN))

        @pl.loop(begun, pick(index, BEGUN))
        def _(ahead):
            begin_unit(ahead)

        had = jnp.where(index == 0, 0, pick(index - 1, NEEDED))
        need = pick(index, NEEDED)
        for more in range(2):

            @pl.when(had + more < need)
            def _():
                take_piece(had + more)

        @pl.when(index == SHARE_AT)
        def _():
            share_weights()

        tile, own_head = pick(index, UNIT_ORDER, 0), pick(index, UNIT_ORDER, 1)
        end_unit(tile, own_head, index)
        for kind in (0, 1):
            gather_copy(tile, own_head, kind).start()
        direct = False
        for i in DIRECT:
            direct = jnp.logical_or(direct, index == i)

        @pl.when(direct)
        def _():
            gather_copy(tile, own_head, 4).start()

        behind = index - LAG
        relayed = behind >= 0
        for i in DIRECT:
            relayed = jnp.logical_and(relayed, behind != i)

        @pl.when(relayed)
        def _():
            relay(pick(behind, UNIT_ORDER, 0), pick(behind, UNIT_ORDER, 1))

        @pl.when(index == PROJECT_AT)
        def _():
            for slot in range(1, heads):
                w_share(slot, others).wait_recv()
            project(0)

    for index in range(PIECES - LAG, PIECES):
        if index not in DIRECT:
            relay(*UNIT_ORDER[index])
    for tile in range(1, tiles):
        project(tile)
    for tile in range(tiles):
        combine(tile)

    for tile in range(tiles):
        rows = pl.ds(tile * TILE, TILE)
        pltpu.make_async_copy(out_v.at[rows], out_hbm.at[rows], out_sem.at[tile]).wait()
        exchange(tile).wait_send()
    for d in range(1, heads):
        w_share(d, mine).wait_send()
        for copy in w_copies(d):
            copy.wait_send()

    @pl.loop(0, PIECES)
    def _(index):
        tile, own_head = pick(index, UNIT_ORDER, 0), pick(index, UNIT_ORDER, 1)
        for kind in (0, 1):
            gather_copy(tile, own_head, kind).wait_send()
        direct = False
        for i in DIRECT:
            direct = jnp.logical_or(direct, index == i)

        @pl.when(direct)
        def _():
            gather_copy(tile, own_head, 4).wait_send()

        @pl.when(jnp.logical_not(direct))
        def _():
            for kind in (2, 3):
                gather_copy(tile, own_head, kind).wait_send()

        @pl.when(has_far)
        def _():
            for copy in far_copies(index):
                copy.wait_send()

    for copy in near_copies:
        copy.wait_send()


def local(queries, keys, values, residual, gate, out_weight, time_offsets, guidance_index):
    rows, features = queries.shape[1:]
    heads = lax.axis_size("head")
    smem = pl.BlockSpec(memory_space=pltpu.SMEM)
    vmem = pl.BlockSpec(memory_space=pltpu.VMEM)
    hbm = pl.BlockSpec(memory_space=pl.ANY)
    block = pltpu.VMEM((rows, features), BF)
    dma = pltpu.SemaphoreType.DMA
    tiles = rows // TILE
    return pl.pallas_call(
        kernel,
        out_shape=jax.ShapeDtypeStruct((rows, features), BF),
        in_specs=[smem, smem, vmem, hbm, hbm, hbm, hbm, hbm],
        out_specs=hbm,
        scratch_shapes=[block] * 7
        + [
            pltpu.VMEM((rows, 2, features), BF),
            pltpu.VMEM((2, rows, features), BF),
            pltpu.VMEM((heads, features, 2 * features), BF),
            pltpu.VMEM((heads, rows, features), BF),
            pltpu.VMEM((TILE, 4 * TILE), F32),
            pltpu.VMEM((PIECES, TILE, HD), F32),
            pltpu.VMEM((PIECES, TILE, 2 * HD), F32),
            pltpu.VMEM((rows, features), F32),
            block,
            block,
            block,
            dma((6,)),
            dma((2,)),
            dma((2,)),
            dma((PIECES, 2)),
            dma((PIECES, 2)),
            dma((heads - 1, 2)),
            dma((heads - 1, 2)),
            dma((heads - 1,)),
            dma((heads - 1,)),
            dma((PIECES, 5)),
            dma((PIECES, 5)),
            dma((tiles,)),
            dma((tiles,)),
            dma((tiles,)),
        ],
        compiler_params=pltpu.CompilerParams(
            collective_id=0, has_side_effects=True, vmem_limit_bytes=VMEM
        ),
        name="block",
    )(time_offsets, guidance_index, gate, queries[0], keys[0], values[0], residual[0], out_weight)


def solution(mesh):
    return jax.shard_map(
        local,
        mesh=mesh,
        in_specs=(
            P("branch", "tokens", "head"),
            P("branch", "tokens", "head"),
            P("branch", "tokens", "head"),
            P("branch", "tokens", None, "head"),
            P(),
            P("head", None),
            P(),
            P(),
        ),
        out_specs=P("tokens", ("branch", "head")),
        check_vma=False,
    )
```

```python
import math

import jax
import jax.numpy as jnp
from jax import lax
from jax.experimental import pallas as pl
from jax.experimental.pallas import tpu as pltpu
from jax.sharding import PartitionSpec as P

HD = 128
TILE = 384
FRAME = 64
BF = jnp.bfloat16
F32 = jnp.float32
SCALE = math.log2(math.e) / math.sqrt(HD)
WINDOWS = (4, 2)
PIECES = 9
VMEM = 62 * 2**20
PIECE_ORDER = ((0, 0), (1, 0), (2, 0), (0, 1), (1, 1), (0, 2), (1, 2), (2, 1), (2, 2))
UNIT_ORDER = ((0, 0), (1, 0), (2, 0), (0, 1), (0, 2), (1, 1), (2, 1), (1, 2), (2, 2))
STEPS = (
    (0, None, None, None),
    (1, 0, None, None),
    (2, 1, 0, None),
    (3, 2, 1, None),
    (None, None, 2, None),
    (4, 3, None, 0),
    (5, 4, 3, 1),
    (6, 5, None, 2),
    (7, 6, 4, 3),
    (8, 7, 5, None),
    (None, None, 6, None),
    (None, 8, 7, None),
    (None, None, 8, None),
)
DIRECT = (4, 5, 7)
HELD = (6, 8)
SHARE_AT = 2
PROJECT_AT = 6


def pick(index, table, field=None):
    found = 0
    for i, entry in enumerate(table):
        value = entry if field is None else entry[field]
        if value:
            found = found + jnp.where(index == i, value, 0)
    return found


def kernel(
    offsets, guidance, gate, q_hbm, k_hbm, v_hbm, r_hbm, w_hbm, own_hbm, came_hbm,
    q_own, k_own, v_own, k_near, v_near, k_far, v_far, res_raw, res, w_all, att, scores, tops, totals,
    own_half, x_send,
    local_sem, near_send, near_recv, halo_send, halo_recv, w_send, w_recv, s_send, s_recv, a_send, a_recv, x_ssem, x_rsem, out_sem,
):
    branch = lax.axis_index("branch")
    head = lax.axis_index("head")
    width = lax.axis_index("tokens")
    widths = lax.axis_size("tokens")
    heads = lax.axis_size("head")
    features = q_own.shape[1]
    local_heads = features // HD
    tiles = q_own.shape[0] // TILE
    half_full = w_hbm.shape[1] // 2
    rows_all = q_own.shape[0]
    step = 1 - 2 * lax.rem(width, 2)
    sibling = width + step
    far = width - step
    has_far = jnp.logical_and(far >= 0, far < widths)
    same_z = lax.rem(width + 1, 4) >= 2
    window = jnp.where(same_z, WINDOWS[0], WINDOWS[1])
    peers = [lax.rem(head + d, heads) for d in range(1, heads)]

    def mine_columns(which, owner):
        half = branch if which == 0 else 1 - branch
        return pl.ds(pl.multiple_of(half * half_full + owner * features, HD), features)

    loads = [
        pltpu.make_async_copy(src, dst, local_sem.at[i])
        for i, (src, dst) in enumerate(
            ((k_hbm, k_own), (v_hbm, v_own), (q_hbm, q_own), (r_hbm, res_raw))
        )
    ] + [
        pltpu.make_async_copy(
            w_hbm.at[:, mine_columns(which, head)],
            w_all.at[0, :, pl.ds(which * features, features)],
            local_sem.at[4 + which],
        )
        for which in range(2)
    ]
    for load in loads:
        load.start()

    barrier = pltpu.get_barrier_semaphore()

    @pl.when(has_far)
    def _():
        pl.semaphore_signal(barrier, inc=1, device_id={"tokens": far})

    pl.semaphore_signal(barrier, inc=1, device_id={"tokens": sibling})
    for peer in peers:
        pl.semaphore_signal(barrier, inc=1, device_id={"head": peer})
    pl.semaphore_signal(barrier, inc=1, device_id={"branch": 1 - branch})
    pl.semaphore_wait(barrier, heads + 1 + has_far.astype(jnp.int32))

    near_copies = [
        pltpu.make_async_remote_copy(
            src_ref=src,
            dst_ref=dst,
            send_sem=near_send.at[i],
            recv_sem=near_recv.at[i],
            device_id={"tokens": sibling},
        )
        for i, (src, dst) in enumerate(((k_hbm, k_near), (v_hbm, v_near)))
    ]

    def piece(index):
        tile, own_head = pick(index, PIECE_ORDER, 0), pick(index, PIECE_ORDER, 1)
        return (
            pl.ds(pl.multiple_of(tile * TILE, TILE), TILE),
            pl.ds(pl.multiple_of(own_head * HD, HD), HD),
        )

    def far_copies(index):
        where = piece(index)
        return [
            pltpu.make_async_remote_copy(
                src_ref=src.at[where],
                dst_ref=dst.at[where],
                send_sem=halo_send.at[index, i],
                recv_sem=halo_recv.at[index, i],
                device_id={"tokens": far},
            )
            for i, (src, dst) in enumerate(((k_hbm, k_far), (v_hbm, v_far)))
        ]

    def send_piece(index):
        @pl.when(has_far)
        def _():
            for copy in far_copies(index):
                copy.start()

    def take_piece(index):
        @pl.when(has_far)
        def _():
            for copy in far_copies(index):
                copy.wait_recv()

        @pl.when(index + window < PIECES)
        def _():
            send_piece(index + window)

    for index in range(max(WINDOWS)):

        @pl.when(index < window)
        def _():
            send_piece(index)


    share = features // 2
    mine = pl.ds(pl.multiple_of(lax.rem(width, 2) * share, share), share)
    others = pl.ds(pl.multiple_of((1 - lax.rem(width, 2)) * share, share), share)

    def w_copies(d):
        return [
            pltpu.make_async_remote_copy(
                src_ref=w_hbm.at[mine, mine_columns(which, peers[d - 1])],
                dst_ref=w_all.at[heads - d, mine, pl.ds(which * features, features)],
                send_sem=w_send.at[d - 1, which],
                recv_sem=w_recv.at[heads - d - 1, which],
                device_id={"head": peers[d - 1]},
            )
            for which in range(2)
        ]

    def w_share(slot, rows):
        return pltpu.make_async_remote_copy(
            src_ref=w_all.at[slot, rows],
            dst_ref=w_all.at[slot, rows],
            send_sem=s_send.at[slot - 1],
            recv_sem=s_recv.at[slot - 1],
            device_id={"tokens": sibling},
        )

    for d in range(1, heads):
        for copy in w_copies(d):
            copy.start()
    for copy in near_copies:
        copy.start()
    for load in loads:
        load.wait()
    for part in range(rows_all // FRAME):
        span = pl.ds(part * FRAME, FRAME)
        both = res_raw[span, :, :].astype(F32)
        for half in range(2):
            res[half, span, :] = both[:, half, :].astype(BF)

    @pl.when(jnp.logical_not(has_far))
    def _():
        k_far[...] = k_own[...]
        v_far[...] = jnp.zeros_like(v_far)

    early = ((k_own, v_own), (k_near, v_near))
    late = ((k_far, v_far),)

    def attend(tile, own_head, columns, present):
        offset = offsets[tile, width]
        back = offset == 1
        second = jnp.where(back, tile - 1, tile + 1)
        valid = jnp.logical_and(second >= 0, second < tiles)
        rows = pl.ds(pl.multiple_of(tile * TILE, TILE), TILE)
        before = pl.ds(pl.multiple_of(jnp.maximum(tile - 1, 0) * TILE, TILE), TILE)
        after = pl.ds(pl.multiple_of(jnp.minimum(tile + 1, tiles - 1) * TILE, TILE), TILE)
        cols = pl.ds(pl.multiple_of(own_head * HD, HD), HD)
        query = q_own[rows, cols]
        top = None
        for i, (k_ref, _) in enumerate(columns):
            for which in range(2):
                if which == 0:
                    key = k_ref[rows, cols]
                else:
                    key = jnp.where(back, k_ref[before, cols], k_ref[after, cols])
                found = lax.dot_general(
                    query, key, (((1,), (1,)), ((), ())), preferred_element_type=F32
                )
                first = (2 * i + which) * TILE
                scores[:, first : first + TILE] = found
                for lane in range(0, TILE, HD):
                    part = found[:, lane : lane + HD]
                    top = part if top is None else jnp.maximum(top, part)
        top = jnp.max(top, axis=1, keepdims=True) * SCALE

        def blend(top):
            total = None
            for i, (_, v_ref) in enumerate(columns):
                for which in range(2):
                    if which == 0:
                        value = v_ref[rows, cols]
                        count = present
                    else:
                        value = jnp.where(back, v_ref[before, cols], v_ref[after, cols])
                        value = jnp.where(valid, value, jnp.zeros_like(value))
                        count = present * valid.astype(F32)
                    ones = jnp.full((TILE, HD), count, F32).astype(BF)
                    first = (2 * i + which) * TILE
                    weights = jnp.exp2(scores[:, first : first + TILE] * SCALE - top).astype(BF)
                    term = jnp.dot(
                        weights,
                        jnp.concatenate([value, ones], axis=1),
                        preferred_element_type=F32,
                    )
                    total = term if total is None else total + term
            return total

        return top, blend

    def begin_unit(index):
        tile, own_head = pick(index, UNIT_ORDER, 0), pick(index, UNIT_ORDER, 1)
        top, blend = attend(tile, own_head, early, jnp.float32(1))
        tops[index] = jnp.broadcast_to(top, (TILE, HD))
        totals[index] = blend(top)

    def end_unit(tile, own_head, index):
        top, blend = attend(tile, own_head, late, has_far.astype(F32))
        old = tops[index][:, :1]
        new = jnp.maximum(old, top)
        total = blend(new) + totals[index] * jnp.exp2(old - new)
        rows = pl.ds(pl.multiple_of(tile * TILE, TILE), TILE)
        cols = pl.ds(pl.multiple_of(own_head * HD, HD), HD)
        att[0, rows, cols] = (total[:, :HD] / total[:, HD:]).astype(BF)

    def gather_copy(tile, own_head, kind):
        forwards = kind % 2 == 0
        own = kind != 2 and kind != 3
        first = tile * TILE + (0 if own or forwards else TILE // 2)
        count = TILE if own else TILE // 2
        where = (
            pl.ds(pl.multiple_of(first, TILE // 2), count),
            pl.ds(pl.multiple_of(own_head * HD, HD), HD),
        )
        came = heads - 1 if forwards else 1
        source = 0 if own else came
        dest = came if kind < 2 else 2
        target = peers[1] if kind == 4 else peers[0] if forwards else peers[-1]
        index = tile * local_heads + own_head
        return pltpu.make_async_remote_copy(
            src_ref=att.at[(source, *where)],
            dst_ref=att.at[(dest, *where)],
            send_sem=a_send.at[index, kind],
            recv_sem=a_recv.at[index, kind],
            device_id={"head": target},
        )

    def relay(tile, own_head):
        for kind in (0, 1):
            gather_copy(tile, own_head, kind).wait_recv()
            gather_copy(tile, own_head, kind + 2).start()

    def share_weights():
        for d in range(1, heads):
            for copy in w_copies(d):
                copy.wait_recv()
        for slot in range(1, heads):
            w_share(slot, mine).start()

    def exchange(tile):
        rows = pl.ds(tile * TILE, TILE)
        return pltpu.make_async_remote_copy(
            src_ref=x_send.at[rows],
            dst_ref=came_hbm.at[rows],
            send_sem=x_ssem.at[tile],
            recv_sem=x_rsem.at[tile],
            device_id={"branch": 1 - branch},
        )

    def own_copy(tile):
        rows = pl.ds(tile * TILE, TILE)
        return pltpu.make_async_copy(own_half.at[rows], own_hbm.at[rows], out_sem.at[tile])

    frames = TILE // FRAME
    gate_cols = pl.ds(pl.multiple_of(head * features, HD), features)

    def project(tile):
        rows = pl.ds(tile * TILE, TILE)
        for own_head in range(local_heads):
            direct = UNIT_ORDER.index((tile, own_head)) in DIRECT
            for kind in (0, 1, 4) if direct else (2, 3):
                gather_copy(tile, own_head, kind).wait_recv()
        for which in (1, 0):
            half = branch if which == 0 else 1 - branch
            lanes = pl.ds(which * features, features)
            summed = None
            for slot in range(heads):
                term = jnp.dot(
                    att[slot, rows, :], w_all[slot, :, lanes], preferred_element_type=F32
                )
                summed = term if summed is None else summed + term
            both = gate[branch, :, gate_cols].astype(F32)
            scale = jnp.where(half == 0, both[0:1], both[1:2])
            hidden = res[half, rows, :].astype(F32) + scale * summed
            for frame in range(frames):
                part = pl.ds(tile * TILE + frame * FRAME, FRAME)
                strength = 1.0 + 0.5 * guidance[tile * frames + frame].astype(F32)
                mine = jnp.where(branch == 0, strength, 1.0 - strength)
                scaled = hidden[frame * FRAME : (frame + 1) * FRAME] * mine
                if which == 1:
                    x_send[part, :] = scaled.astype(BF)
                else:
                    own_half[part, :] = scaled
            if which == 1:
                exchange(tile).start()
            else:
                own_copy(tile).start()

    for copy in near_copies:
        copy.wait_recv()

    def finish(index):
        @pl.when(index == SHARE_AT)
        def _():
            share_weights()

        tile, own_head = pick(index, UNIT_ORDER, 0), pick(index, UNIT_ORDER, 1)
        end_unit(tile, own_head, index)
        held = False
        for i in HELD:
            held = jnp.logical_or(held, index == i)

        @pl.when(jnp.logical_not(held))
        def _():
            for kind in (0, 1):
                gather_copy(tile, own_head, kind).start()

        direct = False
        for i in DIRECT:
            direct = jnp.logical_or(direct, index == i)

        @pl.when(direct)
        def _():
            gather_copy(tile, own_head, 4).start()

        @pl.when(index == PROJECT_AT)
        def _():
            for slot in range(1, heads):
                w_share(slot, others).wait_recv()
            project(0)

    @pl.loop(0, len(STEPS))
    def _(step):
        begun, taken, ended, relayed = (
            pick(step, [0 if entry[i] is None else entry[i] + 1 for entry in STEPS])
            for i in range(4)
        )

        @pl.when(begun > 0)
        def _():
            begin_unit(begun - 1)

        @pl.when(taken > 0)
        def _():
            take_piece(taken - 1)

        @pl.when(ended > 0)
        def _():
            finish(ended - 1)

        @pl.when(relayed > 0)
        def _():
            relay(pick(relayed - 1, UNIT_ORDER, 0), pick(relayed - 1, UNIT_ORDER, 1))

    for kind in (0, 1, 4):
        gather_copy(*UNIT_ORDER[7], kind).wait_send()
    for index in HELD:
        for kind in (0, 1):
            gather_copy(*UNIT_ORDER[index], kind).start()
    project(1)
    for index in HELD:
        relay(*UNIT_ORDER[index])
    project(2)
    for tile in range(tiles):
        own_copy(tile).wait()
        exchange(tile).wait()
    for d in range(1, heads):
        w_share(d, mine).wait_send()
        for copy in w_copies(d):
            copy.wait_send()

    @pl.loop(0, PIECES)
    def _(index):
        tile, own_head = pick(index, UNIT_ORDER, 0), pick(index, UNIT_ORDER, 1)

        @pl.when(index != 7)
        def _():
            for kind in (0, 1):
                gather_copy(tile, own_head, kind).wait_send()

        direct = False
        for i in DIRECT:
            direct = jnp.logical_or(direct, index == i)

        @pl.when(jnp.logical_and(direct, index != 7))
        def _():
            gather_copy(tile, own_head, 4).wait_send()

        @pl.when(jnp.logical_not(direct))
        def _():
            for kind in (2, 3):
                gather_copy(tile, own_head, kind).wait_send()

        @pl.when(has_far)
        def _():
            for copy in far_copies(index):
                copy.wait_send()

    for copy in near_copies:
        copy.wait_send()


def local(queries, keys, values, residual, gate, out_weight, time_offsets, guidance_index):
    rows, features = queries.shape[1:]
    heads = lax.axis_size("head")
    smem = pl.BlockSpec(memory_space=pltpu.SMEM)
    vmem = pl.BlockSpec(memory_space=pltpu.VMEM)
    hbm = pl.BlockSpec(memory_space=pltpu.HBM)
    block = pltpu.VMEM((rows, features), BF)
    dma = pltpu.SemaphoreType.DMA
    tiles = rows // TILE
    own, came = pl.pallas_call(
        kernel,
        out_shape=[
            jax.ShapeDtypeStruct((rows, features), F32),
            jax.ShapeDtypeStruct((rows, features), BF),
        ],
        in_specs=[smem, smem, vmem, hbm, hbm, hbm, hbm, hbm],
        out_specs=[pl.BlockSpec(memory_space=pl.ANY)] * 2,
        scratch_shapes=[block] * 7
        + [
            pltpu.VMEM((rows, 2, features), BF),
            pltpu.VMEM((2, rows, features), BF),
            pltpu.VMEM((heads, features, 2 * features), BF),
            pltpu.VMEM((heads, rows, features), BF),
            pltpu.VMEM((TILE, 4 * TILE), F32),
            pltpu.VMEM((PIECES, TILE, HD), F32),
            pltpu.VMEM((PIECES, TILE, 2 * HD), F32),
            pltpu.VMEM((rows, features), F32),
            block,
            dma((6,)),
            dma((2,)),
            dma((2,)),
            dma((PIECES, 2)),
            dma((PIECES, 2)),
            dma((heads - 1, 2)),
            dma((heads - 1, 2)),
            dma((heads - 1,)),
            dma((heads - 1,)),
            dma((PIECES, 5)),
            dma((PIECES, 5)),
            dma((tiles,)),
            dma((tiles,)),
            dma((tiles,)),
        ],
        compiler_params=pltpu.CompilerParams(
            collective_id=0, has_side_effects=True, vmem_limit_bytes=VMEM
        ),
        name="block",
    )(time_offsets, guidance_index, gate, queries[0], keys[0], values[0], residual[0], out_weight)
    return (own + came.astype(F32)).astype(BF)


def solution(mesh):
    return jax.shard_map(
        local,
        mesh=mesh,
        in_specs=(
            P("branch", "tokens", "head"),
            P("branch", "tokens", "head"),
            P("branch", "tokens", "head"),
            P("branch", "tokens", None, "head"),
            P(),
            P("head", None),
            P(),
            P(),
        ),
        out_specs=P("tokens", ("branch", "head")),
        check_vma=False,
    )
```

```python
import math

import jax
import jax.numpy as jnp
from jax import lax
from jax.experimental import pallas as pl
from jax.experimental.pallas import tpu as pltpu
from jax.sharding import PartitionSpec as P

HD = 128
TILE = 384
FRAME = 64
BF = jnp.bfloat16
F32 = jnp.float32
SCALE = math.log2(math.e) / math.sqrt(HD)
WINDOWS = (5, 3)
PIECES = 9
VMEM = 62 * 2**20
PIECE_ORDER = ((0, 0), (1, 0), (2, 0), (0, 1), (1, 1), (0, 2), (1, 2), (2, 1), (2, 2))
UNIT_ORDER = ((0, 0), (1, 0), (2, 0), (0, 1), (0, 2), (1, 1), (2, 1), (1, 2), (2, 2))
STEPS = (
    (0, None, None, None),
    (1, 0, None, None),
    (2, 1, 0, None),
    (3, 2, 1, None),
    (None, None, 2, None),
    (4, 3, None, 0),
    (5, 4, 3, 1),
    (6, 5, None, 2),
    (7, 6, 4, 3),
    (8, 7, 5, None),
    (None, None, 6, None),
    (None, 8, 7, None),
    (None, None, 8, None),
)
DIRECT = (4, 5, 6, 7, 8)
HELD = ()
SHARE_AT = 2
PROJECT_AT = 6


def pick(index, table, field=None):
    found = 0
    for i, entry in enumerate(table):
        value = entry if field is None else entry[field]
        if value:
            found = found + jnp.where(index == i, value, 0)
    return found


def kernel(
    offsets, guidance, gate, q_hbm, k_hbm, v_hbm, r_hbm, w_hbm, own_hbm, came_hbm,
    q_own, k_own, v_own, k_near, v_near, k_far, v_far, res_raw, res, w_all, att, scores, tops, totals,
    own_half, x_send,
    local_sem, near_send, near_recv, halo_send, halo_recv, w_send, w_recv, s_send, s_recv, a_send, a_recv, x_ssem, x_rsem, out_sem,
):
    branch = lax.axis_index("branch")
    head = lax.axis_index("head")
    width = lax.axis_index("tokens")
    widths = lax.axis_size("tokens")
    heads = lax.axis_size("head")
    features = q_own.shape[1]
    local_heads = features // HD
    tiles = q_own.shape[0] // TILE
    half_full = w_hbm.shape[1] // 2
    rows_all = q_own.shape[0]
    step = 1 - 2 * lax.rem(width, 2)
    sibling = width + step
    far = width - step
    has_far = jnp.logical_and(far >= 0, far < widths)
    same_z = lax.rem(width + 1, 4) >= 2
    window = jnp.where(same_z, WINDOWS[0], WINDOWS[1])
    peers = [lax.rem(head + d, heads) for d in range(1, heads)]

    def mine_columns(which, owner):
        half = branch if which == 0 else 1 - branch
        return pl.ds(pl.multiple_of(half * half_full + owner * features, HD), features)

    loads = [
        pltpu.make_async_copy(src, dst, local_sem.at[i])
        for i, (src, dst) in enumerate(
            ((k_hbm, k_own), (v_hbm, v_own), (q_hbm, q_own), (r_hbm, res_raw))
        )
    ] + [
        pltpu.make_async_copy(
            w_hbm.at[:, mine_columns(which, head)],
            w_all.at[0, :, pl.ds(which * features, features)],
            local_sem.at[4 + which],
        )
        for which in range(2)
    ]
    for load in loads:
        load.start()

    barrier = pltpu.get_barrier_semaphore()

    @pl.when(has_far)
    def _():
        pl.semaphore_signal(barrier, inc=1, device_id={"tokens": far})

    pl.semaphore_signal(barrier, inc=1, device_id={"tokens": sibling})
    for peer in peers:
        pl.semaphore_signal(barrier, inc=1, device_id={"head": peer})
    pl.semaphore_signal(barrier, inc=1, device_id={"branch": 1 - branch})
    pl.semaphore_wait(barrier, heads + 1 + has_far.astype(jnp.int32))

    near_copies = [
        pltpu.make_async_remote_copy(
            src_ref=src,
            dst_ref=dst,
            send_sem=near_send.at[i],
            recv_sem=near_recv.at[i],
            device_id={"tokens": sibling},
        )
        for i, (src, dst) in enumerate(((k_hbm, k_near), (v_hbm, v_near)))
    ]

    def piece(index):
        tile, own_head = pick(index, PIECE_ORDER, 0), pick(index, PIECE_ORDER, 1)
        return (
            pl.ds(pl.multiple_of(tile * TILE, TILE), TILE),
            pl.ds(pl.multiple_of(own_head * HD, HD), HD),
        )

    def far_copies(index):
        where = piece(index)
        return [
            pltpu.make_async_remote_copy(
                src_ref=src.at[where],
                dst_ref=dst.at[where],
                send_sem=halo_send.at[index, i],
                recv_sem=halo_recv.at[index, i],
                device_id={"tokens": far},
            )
            for i, (src, dst) in enumerate(((k_hbm, k_far), (v_hbm, v_far)))
        ]

    def send_piece(index):
        @pl.when(has_far)
        def _():
            for copy in far_copies(index):
                copy.start()

    def take_piece(index):
        @pl.when(has_far)
        def _():
            for copy in far_copies(index):
                copy.wait_recv()

        @pl.when(index + window < PIECES)
        def _():
            send_piece(index + window)

    for index in range(max(WINDOWS)):

        @pl.when(index < window)
        def _():
            send_piece(index)


    share = features // 2
    mine = pl.ds(pl.multiple_of(lax.rem(width, 2) * share, share), share)
    others = pl.ds(pl.multiple_of((1 - lax.rem(width, 2)) * share, share), share)

    def w_copies(d):
        return [
            pltpu.make_async_remote_copy(
                src_ref=w_hbm.at[mine, mine_columns(which, peers[d - 1])],
                dst_ref=w_all.at[heads - d, mine, pl.ds(which * features, features)],
                send_sem=w_send.at[d - 1, which],
                recv_sem=w_recv.at[heads - d - 1, which],
                device_id={"head": peers[d - 1]},
            )
            for which in range(2)
        ]

    def w_share(slot, rows):
        return pltpu.make_async_remote_copy(
            src_ref=w_all.at[slot, rows],
            dst_ref=w_all.at[slot, rows],
            send_sem=s_send.at[slot - 1],
            recv_sem=s_recv.at[slot - 1],
            device_id={"tokens": sibling},
        )

    for d in range(1, heads):
        for copy in w_copies(d):
            copy.start()
    for copy in near_copies:
        copy.start()
    for load in loads:
        load.wait()
    for part in range(rows_all // FRAME):
        span = pl.ds(part * FRAME, FRAME)
        both = res_raw[span, :, :].astype(F32)
        for half in range(2):
            res[half, span, :] = both[:, half, :].astype(BF)

    @pl.when(jnp.logical_not(has_far))
    def _():
        k_far[...] = k_own[...]
        v_far[...] = jnp.zeros_like(v_far)

    early = ((k_own, v_own), (k_near, v_near))
    late = ((k_far, v_far),)

    def attend(tile, own_head, columns, present):
        offset = offsets[tile, width]
        back = offset == 1
        second = jnp.where(back, tile - 1, tile + 1)
        valid = jnp.logical_and(second >= 0, second < tiles)
        rows = pl.ds(pl.multiple_of(tile * TILE, TILE), TILE)
        before = pl.ds(pl.multiple_of(jnp.maximum(tile - 1, 0) * TILE, TILE), TILE)
        after = pl.ds(pl.multiple_of(jnp.minimum(tile + 1, tiles - 1) * TILE, TILE), TILE)
        cols = pl.ds(pl.multiple_of(own_head * HD, HD), HD)
        query = q_own[rows, cols]
        top = None
        for i, (k_ref, _) in enumerate(columns):
            for which in range(2):
                if which == 0:
                    key = k_ref[rows, cols]
                else:
                    key = jnp.where(back, k_ref[before, cols], k_ref[after, cols])
                found = lax.dot_general(
                    query, key, (((1,), (1,)), ((), ())), preferred_element_type=F32
                )
                first = (2 * i + which) * TILE
                scores[:, first : first + TILE] = found
                for lane in range(0, TILE, HD):
                    part = found[:, lane : lane + HD]
                    top = part if top is None else jnp.maximum(top, part)
        top = jnp.max(top, axis=1, keepdims=True) * SCALE

        def blend(top):
            total = None
            for i, (_, v_ref) in enumerate(columns):
                for which in range(2):
                    if which == 0:
                        value = v_ref[rows, cols]
                        count = present
                    else:
                        value = jnp.where(back, v_ref[before, cols], v_ref[after, cols])
                        value = jnp.where(valid, value, jnp.zeros_like(value))
                        count = present * valid.astype(F32)
                    ones = jnp.full((TILE, HD), count, F32).astype(BF)
                    first = (2 * i + which) * TILE
                    weights = jnp.exp2(scores[:, first : first + TILE] * SCALE - top).astype(BF)
                    term = jnp.dot(
                        weights,
                        jnp.concatenate([value, ones], axis=1),
                        preferred_element_type=F32,
                    )
                    total = term if total is None else total + term
            return total

        return top, blend

    def begin_unit(index):
        tile, own_head = pick(index, UNIT_ORDER, 0), pick(index, UNIT_ORDER, 1)
        top, blend = attend(tile, own_head, early, jnp.float32(1))
        tops[index] = jnp.broadcast_to(top, (TILE, HD))
        totals[index] = blend(top)

    def end_unit(tile, own_head, index):
        top, blend = attend(tile, own_head, late, has_far.astype(F32))
        old = tops[index][:, :1]
        new = jnp.maximum(old, top)
        total = blend(new) + totals[index] * jnp.exp2(old - new)
        rows = pl.ds(pl.multiple_of(tile * TILE, TILE), TILE)
        cols = pl.ds(pl.multiple_of(own_head * HD, HD), HD)
        att[0, rows, cols] = (total[:, :HD] / total[:, HD:]).astype(BF)

    def gather_copy(tile, own_head, kind):
        forwards = kind % 2 == 0
        own = kind != 2 and kind != 3
        first = tile * TILE + (0 if own or forwards else TILE // 2)
        count = TILE if own else TILE // 2
        where = (
            pl.ds(pl.multiple_of(first, TILE // 2), count),
            pl.ds(pl.multiple_of(own_head * HD, HD), HD),
        )
        came = heads - 1 if forwards else 1
        source = 0 if own else came
        dest = came if kind < 2 else 2
        target = peers[1] if kind == 4 else peers[0] if forwards else peers[-1]
        index = tile * local_heads + own_head
        return pltpu.make_async_remote_copy(
            src_ref=att.at[(source, *where)],
            dst_ref=att.at[(dest, *where)],
            send_sem=a_send.at[index, kind],
            recv_sem=a_recv.at[index, kind],
            device_id={"head": target},
        )

    def relay(tile, own_head):
        for kind in (0, 1):
            gather_copy(tile, own_head, kind).wait_recv()
            gather_copy(tile, own_head, kind + 2).start()

    def share_weights():
        for d in range(1, heads):
            for copy in w_copies(d):
                copy.wait_recv()
        for slot in range(1, heads):
            w_share(slot, mine).start()

    def exchange(tile):
        rows = pl.ds(tile * TILE, TILE)
        return pltpu.make_async_remote_copy(
            src_ref=x_send.at[rows],
            dst_ref=came_hbm.at[rows],
            send_sem=x_ssem.at[tile],
            recv_sem=x_rsem.at[tile],
            device_id={"branch": 1 - branch},
        )

    def own_copy(tile):
        rows = pl.ds(tile * TILE, TILE)
        return pltpu.make_async_copy(own_half.at[rows], own_hbm.at[rows], out_sem.at[tile])

    frames = TILE // FRAME
    gate_cols = pl.ds(pl.multiple_of(head * features, HD), features)

    def project(tile):
        rows = pl.ds(tile * TILE, TILE)
        for own_head in range(local_heads):
            direct = UNIT_ORDER.index((tile, own_head)) in DIRECT
            for kind in (0, 1, 4) if direct else (2, 3):
                gather_copy(tile, own_head, kind).wait_recv()
        for which in (1, 0):
            half = branch if which == 0 else 1 - branch
            lanes = pl.ds(which * features, features)
            summed = None
            for slot in range(heads):
                term = jnp.dot(
                    att[slot, rows, :], w_all[slot, :, lanes], preferred_element_type=F32
                )
                summed = term if summed is None else summed + term
            both = gate[branch, :, gate_cols].astype(F32)
            scale = jnp.where(half == 0, both[0:1], both[1:2])
            hidden = res[half, rows, :].astype(F32) + scale * summed
            for frame in range(frames):
                part = pl.ds(tile * TILE + frame * FRAME, FRAME)
                strength = 1.0 + 0.5 * guidance[tile * frames + frame].astype(F32)
                mine = jnp.where(branch == 0, strength, 1.0 - strength)
                scaled = hidden[frame * FRAME : (frame + 1) * FRAME] * mine
                if which == 1:
                    x_send[part, :] = scaled.astype(BF)
                else:
                    own_half[part, :] = scaled
            if which == 1:
                exchange(tile).start()
            else:
                own_copy(tile).start()

    for copy in near_copies:
        copy.wait_recv()

    def finish(index):
        @pl.when(index == SHARE_AT)
        def _():
            share_weights()

        tile, own_head = pick(index, UNIT_ORDER, 0), pick(index, UNIT_ORDER, 1)
        end_unit(tile, own_head, index)
        held = False
        for i in HELD:
            held = jnp.logical_or(held, index == i)

        @pl.when(jnp.logical_not(held))
        def _():
            for kind in (0, 1):
                gather_copy(tile, own_head, kind).start()

        direct = False
        for i in DIRECT:
            direct = jnp.logical_or(direct, index == i)

        @pl.when(direct)
        def _():
            gather_copy(tile, own_head, 4).start()

        @pl.when(index == PROJECT_AT)
        def _():
            for slot in range(1, heads):
                w_share(slot, others).wait_recv()
            project(0)

    @pl.loop(0, len(STEPS))
    def _(step):
        begun, taken, ended, relayed = (
            pick(step, [0 if entry[i] is None else entry[i] + 1 for entry in STEPS])
            for i in range(4)
        )

        @pl.when(begun > 0)
        def _():
            begin_unit(begun - 1)

        @pl.when(taken > 0)
        def _():
            take_piece(taken - 1)

        @pl.when(ended > 0)
        def _():
            finish(ended - 1)

        @pl.when(relayed > 0)
        def _():
            relay(pick(relayed - 1, UNIT_ORDER, 0), pick(relayed - 1, UNIT_ORDER, 1))

    for kind in (0, 1, 4):
        gather_copy(*UNIT_ORDER[7], kind).wait_send()
    for index in HELD:
        for kind in (0, 1):
            gather_copy(*UNIT_ORDER[index], kind).start()
    project(1)
    for index in HELD:
        relay(*UNIT_ORDER[index])
    project(2)
    for tile in range(tiles):
        own_copy(tile).wait()
        exchange(tile).wait()
    for d in range(1, heads):
        w_share(d, mine).wait_send()
        for copy in w_copies(d):
            copy.wait_send()

    @pl.loop(0, PIECES)
    def _(index):
        tile, own_head = pick(index, UNIT_ORDER, 0), pick(index, UNIT_ORDER, 1)

        @pl.when(index != 7)
        def _():
            for kind in (0, 1):
                gather_copy(tile, own_head, kind).wait_send()

        direct = False
        for i in DIRECT:
            direct = jnp.logical_or(direct, index == i)

        @pl.when(jnp.logical_and(direct, index != 7))
        def _():
            gather_copy(tile, own_head, 4).wait_send()

        @pl.when(jnp.logical_not(direct))
        def _():
            for kind in (2, 3):
                gather_copy(tile, own_head, kind).wait_send()

        @pl.when(has_far)
        def _():
            for copy in far_copies(index):
                copy.wait_send()

    for copy in near_copies:
        copy.wait_send()


def local(queries, keys, values, residual, gate, out_weight, time_offsets, guidance_index):
    rows, features = queries.shape[1:]
    heads = lax.axis_size("head")
    smem = pl.BlockSpec(memory_space=pltpu.SMEM)
    vmem = pl.BlockSpec(memory_space=pltpu.VMEM)
    hbm = pl.BlockSpec(memory_space=pltpu.HBM)
    block = pltpu.VMEM((rows, features), BF)
    dma = pltpu.SemaphoreType.DMA
    tiles = rows // TILE
    own, came = pl.pallas_call(
        kernel,
        out_shape=[
            jax.ShapeDtypeStruct((rows, features), F32),
            jax.ShapeDtypeStruct((rows, features), BF),
        ],
        in_specs=[smem, smem, vmem, hbm, hbm, hbm, hbm, hbm],
        out_specs=[pl.BlockSpec(memory_space=pl.ANY)] * 2,
        scratch_shapes=[block] * 7
        + [
            pltpu.VMEM((rows, 2, features), BF),
            pltpu.VMEM((2, rows, features), BF),
            pltpu.VMEM((heads, features, 2 * features), BF),
            pltpu.VMEM((heads, rows, features), BF),
            pltpu.VMEM((TILE, 4 * TILE), F32),
            pltpu.VMEM((PIECES, TILE, HD), F32),
            pltpu.VMEM((PIECES, TILE, 2 * HD), F32),
            pltpu.VMEM((rows, features), F32),
            block,
            dma((6,)),
            dma((2,)),
            dma((2,)),
            dma((PIECES, 2)),
            dma((PIECES, 2)),
            dma((heads - 1, 2)),
            dma((heads - 1, 2)),
            dma((heads - 1,)),
            dma((heads - 1,)),
            dma((PIECES, 5)),
            dma((PIECES, 5)),
            dma((tiles,)),
            dma((tiles,)),
            dma((tiles,)),
        ],
        compiler_params=pltpu.CompilerParams(
            collective_id=0, has_side_effects=True, vmem_limit_bytes=VMEM
        ),
        name="block",
    )(time_offsets, guidance_index, gate, queries[0], keys[0], values[0], residual[0], out_weight)
    return (own + came.astype(F32)).astype(BF)


def solution(mesh):
    return jax.shard_map(
        local,
        mesh=mesh,
        in_specs=(
            P("branch", "tokens", "head"),
            P("branch", "tokens", "head"),
            P("branch", "tokens", "head"),
            P("branch", "tokens", None, "head"),
            P(),
            P("head", None),
            P(),
            P(),
        ),
        out_specs=P("tokens", ("branch", "head")),
        check_vma=False,
    )
```
